256 devices in a mesh: section: 32 (over z, x_hi, core), tp: 4 (over y), dp: 2 (over x_lo).
Axes of the slice: x: 4 (x_hi: 2, x_lo: 2; x = x_hi * 2 + x_lo), y: 4, z: 8, core: 2. Of those that a mesh axis runs over, the one named last changes fastest.
Arguments:
- held: bfloat16 [32, 2, 128, 8192], P('section', 'dp', None, 'tp'), may hold values from -6 to 6
- incoming: bfloat16 [1, 2, 128, 8192], P(None, 'dp', None, 'tp'), may hold values from -6 to 6
- w_qkv: bfloat16 [32, 8192, 1536], P('section', None, 'tp'), may hold values from -0.0625 to 0.0625
- w_out: bfloat16 [32, 512, 8192], P('section', 'tp'), may hold values from -0.25 to 0.25
- norm_gain: bfloat16 [32, 8192], P('section'), may hold values from 0.099609375 to 1.8984375
Outputs:
- section_out: bfloat16 [2, 32, 2, 128, 8192], P(None, 'section', 'dp', None, 'tp')
- shadow_out: bfloat16 [2, 32, 2, 128, 8192], P(None, 'section', 'dp', None, 'tp')
The draws below stay inside these ranges and needn't reach their ends.
All inputs are finite; a program needn't handle non-finite values.
Results may differ from the reference program's by a relative error of at most 0.014.
Values may be sent and summed in bfloat16 or wider, within the bound.
A program may use at most 128 MiB of HBM per device.

```python
import jax
import jax.numpy as jnp
from jax import lax

D = 8192
HD = 128
HEADS = 4
SEQ_LEN = 128
TICKS = 2
SECTIONS = 32
BATCH = 2


def block_levels(own_key, dims, pieces, least, high):
    factor_of = 1.0
    for position, blocks in pieces:
        steps = jax.random.uniform(jax.random.fold_in(jax.random.fold_in(own_key, 6), position), (blocks,), jnp.float32, least / len(pieces), high / len(pieces))
        factor_of = factor_of * jnp.repeat(jnp.exp(steps), dims[position] // blocks).reshape((-1,) + (1,) * (len(dims) - 1 - position))
    return factor_of


def normal_values(stream_key, dims, scale, bound, cuts=(), held_as=jnp.bfloat16):
    values = jax.random.normal(stream_key, dims, jnp.float32) * scale
    if len(cuts) > 0:
        values = block_levels(stream_key, dims, cuts, -0.22, 0.18) * values
    return jnp.clip(values, min=-bound, max=bound).astype(held_as)


def setup_inputs(seed: int = 0) -> dict:
    streams_of = jax.random.split(jax.random.key(seed), 6)
    return {
        "held": normal_values(streams_of[0], (SECTIONS, BATCH, SEQ_LEN, D), 1.0, 6.0, ((0, 32), (1, 2), (3, 4))),
        "incoming": normal_values(streams_of[1], (TICKS - 1, BATCH, SEQ_LEN, D), 1.0, 6.0, ((1, 2), (3, 4))),
        "w_qkv": normal_values(streams_of[2], (SECTIONS, D, HEADS * 3 * HD), D ** -0.5, 0.0625, ((0, 32), (2, 4))),
        "w_out": normal_values(streams_of[3], (SECTIONS, HEADS * HD, D), (HEADS * HD) ** -0.5, 0.25, ((0, 32), (1, 4))),
        "norm_gain": jnp.clip(1.0 + 0.18 * jax.random.normal(streams_of[4], (SECTIONS, D), jnp.float32), 0.099609375, 1.8984375).astype(jnp.bfloat16),
    }


EPS = 1e-05

def layer(source, w_proj, w_out, gain_row):
    batch, length, width = source.shape
    heads = w_proj.shape[1] // (3 * HD)
    values = source.astype(jnp.float32)
    scale = lax.rsqrt(lax.optimization_barrier(jnp.mean(values * values, axis=-1, keepdims=True)) + EPS)
    normed = (values * scale * gain_row.astype(jnp.float32)).astype(jnp.bfloat16)
    proj = jnp.dot(normed.reshape(batch * length, width), w_proj, preferred_element_type=jnp.float32)
    proj = proj.astype(jnp.bfloat16).reshape(batch, length, heads, 3, HD)
    query = proj[:, :, :, 0].astype(jnp.float32)
    key = proj[:, :, :, 1].astype(jnp.float32)
    value = proj[:, :, :, 2].astype(jnp.float32)
    scores = jnp.einsum('blhe,bmhe->bhlm', query, key) * HD ** (-0.5)
    causal = jnp.arange(length)[:, None] >= jnp.arange(length)[None, :]
    scores = jnp.where(causal[None, None], scores, -1e+30)
    weights = jax.nn.softmax(scores, axis=-1).astype(jnp.bfloat16)
    mixed = jnp.einsum('bhlm,bmhe->blhe', weights.astype(jnp.float32), value)
    mixed = mixed.astype(jnp.bfloat16).reshape(batch * length, heads * HD)
    delta = jnp.dot(mixed, w_out, preferred_element_type=jnp.float32).reshape(batch, length, width)
    return (values + delta).astype(jnp.bfloat16)

def reference(held, incoming, w_qkv, w_out, norm_gain):
    sections = held.shape[0]
    indices = jnp.arange(sections, dtype=jnp.int32)
    current = held
    outputs = []
    shadows = []
    for tick in range(TICKS):

        def own_layer(index, source=current):
            return layer(source[index], w_qkv[index], w_out[index], norm_gain[index])
        result = lax.map(own_layer, indices)

        def next_layer(index, source=result):
            after = ((index + 1) % sections).astype(jnp.int32)
            return layer(source[index], w_qkv[after], w_out[after], norm_gain[after])
        shadow = lax.map(next_layer, indices)
        outputs.append(result)
        shadows.append(shadow)
        if tick + 1 < TICKS:
            current = jnp.concatenate([incoming[tick][None], result[:-1]], axis=0)
    return (jnp.stack(outputs), jnp.stack(shadows))
```

```python
import functools

import jax
import jax.numpy as jnp
from jax import lax
from jax.experimental import pallas as pl
from jax.experimental.pallas import tpu as pltpu
from jax.sharding import PartitionSpec as P

HD = 128
EPS = 1e-05
ROWS = 64
STAGES = 8
MESH = pl.DeviceIdType.MESH


def kernel(
    held, incoming, w_qkv, w_out, gain, sec_out, sh_out,
    w_ref, wo, xg, mg, ob, keys, vals, g32, acc, ssq,
    w_sem, x_sem, wol_sem, wo_s, wo_r, wx_s, wx_r,
    own_s, own_r, fw_s, fw_r, mix_s, mix_r, hop_s, hop_r, ret_s, ret_r, loc_s, inc_s, inc_r,
):
    s, y, d = lax.axis_index("section"), lax.axis_index("tp"), lax.axis_index("dp")
    sections, tps = lax.axis_size("section"), 4
    half_cols = xg.shape[4]
    cols = 2 * half_cols

    def tp(o):
        return lax.rem(y + o, tps)

    right, left = {"tp": tp(1)}, {"tp": tp(3)}
    after = {"section": lax.rem(s + 1, sections)}
    before = {"section": lax.rem(s + sections - 1, sections)}

    def remote(src, dst, send, recv, to):
        return pltpu.make_async_remote_copy(
            src_ref=src, dst_ref=dst, send_sem=send, recv_sem=recv, device_id=to, device_id_type=MESH
        )

    own_rows = pl.ds(pl.multiple_of(y * HD, HD), HD)
    own_cols = pl.ds(pl.multiple_of(y * cols, cols), cols)
    wol = pltpu.make_async_copy(w_out.at[0, :, own_cols], wo.at[own_rows, :], wol_sem)

    def w_load(o):
        block = tp(o)
        rows = pl.ds(pl.multiple_of(block * cols, cols), cols)
        return pltpu.make_async_copy(w_qkv.at[0, rows, :], w_ref.at[rows, :], w_sem.at[o])

    def x_load(k, c):
        return pltpu.make_async_copy(
            held.at[0, 0, pl.ds(k * ROWS, ROWS), pl.ds(c * half_cols, half_cols)], xg.at[k, y, c], x_sem.at[k, c]
        )

    for k in range(2):
        for c in range(2):
            x_load(k, c).start()
    for o in (0, 3, 1, 2):
        w_load(o).start()
    wol.start()

    helper = lax.rem(s, 4) == 0
    barrier = pltpu.get_barrier_semaphore()
    for to in ({"tp": tp(1)}, {"tp": tp(2)}, {"tp": tp(3)}, {"dp": 1 - d}, after, before):
        pl.semaphore_signal(barrier, inc=1, device_id=to, device_id_type=MESH)

    @pl.when(s == 0)
    def _():
        for j in range(1, 8):
            for o in range(4):
                pl.semaphore_signal(barrier, inc=1, device_id={"section": 4 * j, "tp": tp(o)}, device_id_type=MESH)

    pl.semaphore_wait(barrier, jnp.where(jnp.logical_and(helper, s > 0), 10, 6))

    def wo_send(o):
        there = pl.ds(pl.multiple_of(tp(o) * cols, cols), cols)
        mine = pl.ds(pl.multiple_of(y * HD + d * 64, 64), 64)
        return remote(
            w_out.at[0, pl.ds(pl.multiple_of(d * 64, 64), 64), there], wo.at[mine, :], wo_s.at[o], wo_r.at[o], {"tp": tp(o)}
        )

    def wo_pass(o):
        rows = pl.ds(pl.multiple_of(tp(4 - o) * HD + d * 64, 64), 64)
        return remote(wo.at[rows, :], wo.at[rows, :], wx_s.at[o], wx_r.at[o], {"dp": 1 - d})

    for o in (1, 3, 2):
        wo_send(o).start()

    def own_copy(k, way, c, src=None):
        block = xg.at[k, y, c]
        return remote(
            block if src is None else src, block, own_s.at[k, way, c], own_r.at[k, way, c], (right, left)[way]
        )

    def own_arrival(k, way, c):
        block = xg.at[k, tp(3 if way == 0 else 1), c]
        return remote(block, block, own_s.at[k, way, c], own_r.at[k, way, c], (right, left)[way])

    def pass_on(k, way):
        block = xg.at[k, tp(3 if way == 0 else 1), way]
        return remote(block, block, fw_s.at[k, way], fw_r.at[k, way], (right, left)[way])

    def pass_arrival(k, way):
        block = xg.at[k, tp(2), way]
        return remote(block, block, fw_s.at[k, way], fw_r.at[k, way], (right, left)[way])

    for k in range(2):
        for way, c in ((0, 0), (1, 1), (0, 1), (1, 0)):
            own_copy(
                k, way, c, held.at[0, 0, pl.ds(k * ROWS, ROWS), pl.ds(c * half_cols, half_cols)]
            ).start()

    def inc_parts(h, o):
        j = s // 4
        piece = 2 * half_cols // 8
        src = incoming.at[0, 0, pl.ds(h * ROWS, ROWS), pl.ds(pl.multiple_of(j * piece, piece), piece)]
        dst = xg.at[2 + h, y, j // 4, :, pl.ds(pl.multiple_of(lax.rem(j, 4) * piece, piece), piece)]
        return src, dst

    def inc_remote(h, o):
        src, dst = inc_parts(h, o)
        return remote(src, dst, inc_s.at[h, o], inc_r.at[h], {"section": 0, "tp": tp(o)})

    def inc_local(h):
        src, dst = inc_parts(h, 0)
        return pltpu.make_async_copy(src, dst, inc_r.at[h])

    @pl.when(helper)
    def _():
        for h in range(2):
            for o in (1, 2, 3):
                inc_remote(h, o).start()

            @pl.when(s > 0)
            def _():
                inc_remote(h, 0).start()

            @pl.when(s == 0)
            def _():
                inc_local(h).start()

    for i in range(8):
        g32[i] = gain[:, i * half_cols:(i + 1) * half_cols].astype(jnp.float32)
    keys[...] = jnp.zeros_like(keys)
    vals[...] = jnp.zeros_like(vals)

    for o in (1, 3, 2):
        wo_send(o).wait_recv()
        wo_pass(o).start()

    def mix_copy(k, o):
        block = mg.at[k, :, pl.ds(pl.multiple_of(y * HD, HD), HD)]
        return remote(block, block, mix_s.at[k, o - 1], mix_r.at[k, o - 1], {"tp": tp(o)})

    def hop(k, c):
        to = jnp.where(k < 4, k + 4, k + 2)
        return remote(ob.at[k, c], xg.at[to, y, c], hop_s.at[k, c], hop_r.at[to, c], after)

    def hop_arrival(k, c):
        return remote(xg.at[k, y, c], xg.at[k, y, c], hop_s.at[k, c], hop_r.at[k, c], after)

    def out_at(ref, t, k, c):
        rows = pl.ds(pl.multiple_of(lax.rem(k, 2) * ROWS, ROWS), ROWS)
        return ref.at[t, 0, 0, rows, pl.ds(c * half_cols, half_cols)]

    def give_back(k, c):
        t = jnp.where(k < 6, 0, 1)
        return remote(ob.at[k, c], out_at(sh_out, t, k, c), ret_s.at[k, c], ret_r.at[k, c], before)

    def keep(k, c):
        t = jnp.where(k < 2, 0, 1)
        return pltpu.make_async_copy(ob.at[k, c], out_at(sec_out, t, k, c), loc_s.at[k, c])

    def goes_on(k):
        return jnp.logical_or(k < 4, jnp.logical_and(k < 6, s > 0))

    def multiply(k, block, c, first=False):
        index = block * 2 + c
        values = xg[k, block, c].astype(jnp.float32)
        rows = pl.ds(pl.multiple_of(index * half_cols, half_cols), half_cols)
        product = jnp.dot(
            (values * g32[index]).astype(jnp.bfloat16), w_ref[rows, :], preferred_element_type=jnp.float32
        )
        squares = values * values
        part = squares[:, :HD]
        for i in range(1, half_cols // HD):
            part = part + squares[:, i * HD:(i + 1) * HD]
        if first:
            acc[...] = product
            ssq[...] = part
        else:
            acc[...] += product
            ssq[...] += part

    def stage(k):
        gathered = jnp.logical_or(k < 2, k >= 4)

        @pl.when(k < 2)
        def _():
            for c in range(2):
                x_load(k, c).wait()

        @pl.when(k == 0)
        def _():
            for o in range(4):
                w_load(o).wait()

        @pl.when(jnp.logical_not(gathered))
        def _():
            pltpu.make_async_copy(xg.at[k], xg.at[k], inc_r.at[k - 2]).wait()

        multiply(k, y, 0, True)
        multiply(k, y, 1)
        for way in range(2):
            @pl.when(gathered)
            def _():
                own_arrival(k, way, way).wait_recv()
                pass_on(k, way).start()

            multiply(k, tp(3 if way == 0 else 1), way)
        for way in range(2):
            @pl.when(gathered)
            def _():
                own_arrival(k, way, 1 - way).wait_recv()

            multiply(k, tp(3 if way == 0 else 1), 1 - way)
        for way in range(2):
            @pl.when(gathered)
            def _():
                pass_arrival(k, way).wait_recv()

            multiply(k, tp(2), way)

        half = lax.rem(k, 2)
        mean = jnp.sum(ssq[...], axis=1, keepdims=True) * (1.0 / (4 * cols))
        proj = (acc[...] * lax.rsqrt(mean + EPS)).astype(jnp.bfloat16)
        rows = pl.ds(pl.multiple_of(half * ROWS, ROWS), ROWS)
        keys[rows, :] = proj[:, HD:2 * HD]
        vals[rows, :] = proj[:, 2 * HD:]
        scores = lax.dot_general(
            proj[:, :HD], keys[...], (((1,), (1,)), ((), ())), preferred_element_type=jnp.float32
        ) * HD ** (-0.5)
        at_row = lax.broadcasted_iota(jnp.int32, scores.shape, 0) + half * ROWS
        at_col = lax.broadcasted_iota(jnp.int32, scores.shape, 1)
        scores = jnp.where(at_col <= at_row, scores, -1e30)
        powers = jnp.exp(scores - jnp.max(scores, axis=1, keepdims=True))
        weights = (powers / jnp.sum(powers, axis=1, keepdims=True)).astype(jnp.bfloat16)
        mixed = jnp.dot(weights, vals[...], preferred_element_type=jnp.float32).astype(jnp.bfloat16)
        mg[k, :, pl.ds(pl.multiple_of(y * HD, HD), HD)] = mixed
        for o in (2, 1, 3):
            mix_copy(k, o).start()

        @pl.when(jnp.logical_and(gathered, jnp.logical_and(k > 0, k < 7)))
        def _():
            nxt = jnp.where(k == 1, 4, k + 1)
            hop_arrival(nxt, 0).wait_recv()
            own_copy(nxt, 0, 0).start()
            hop_arrival(nxt, 1).wait_recv()
            own_copy(nxt, 1, 1).start()
            own_copy(nxt, 0, 1).start()
            own_copy(nxt, 1, 0).start()

        @pl.when(k == 0)
        def _():
            wol.wait()
            for o in (1, 3, 2):
                wo_pass(o).wait_recv()

        for o in (1, 3, 2):
            mix_copy(k, o).wait_recv()
        mixes = mg[k]
        for c in range(2):
            for i in range(2):
                n = half_cols // 2
                delta = jnp.dot(
                    mixes, wo[:, c * half_cols + i * n:c * half_cols + (i + 1) * n], preferred_element_type=jnp.float32
                )
                ob[k, c, :, i * n:(i + 1) * n] = (
                    xg[k, y, c, :, i * n:(i + 1) * n].astype(jnp.float32) + delta
                ).astype(jnp.bfloat16)

            @pl.when(goes_on(k))
            def _():
                hop(k, c).start()
                keep(k, c).start()

            @pl.when(k >= 4)
            def _():
                give_back(k, c).start()

    def step(k, carry):
        @pl.when(jnp.logical_or(jnp.logical_or(k < 2, k >= 4), s == 0))
        def _():
            stage(k)

        return carry

    lax.fori_loop(0, STAGES, step, 0)

    for o in (1, 3, 2):
        wo_send(o).wait_send()
        wo_pass(o).wait_send()

    @pl.when(helper)
    def _():
        for h in range(2):
            for o in (1, 2, 3):
                inc_remote(h, o).wait_send()

            @pl.when(s > 0)
            def _():
                inc_remote(h, 0).wait_send()

    def drain(k, carry):
        gathered = jnp.logical_or(k < 2, k >= 4)

        @pl.when(gathered)
        def _():
            for way in range(2):
                for c in range(2):
                    own_copy(k, way, c).wait_send()
                pass_on(k, way).wait_send()

        @pl.when(jnp.logical_or(gathered, s == 0))
        def _():
            for o in (1, 2, 3):
                mix_copy(k, o).wait_send()

            @pl.when(goes_on(k))
            def _():
                for c in range(2):
                    hop(k, c).wait_send()
                    keep(k, c).wait()

        @pl.when(k >= 4)
        def _():
            for c in range(2):
                give_back(k, c).wait()

        return carry

    lax.fori_loop(0, STAGES, drain, 0)


def local(held, incoming, w_qkv, w_out, norm_gain):
    cols = held.shape[3]
    half_cols = cols // 2
    outs = jax.ShapeDtypeStruct((2, 1, 1, held.shape[2], cols), jnp.bfloat16)
    anywhere = pl.BlockSpec(memory_space=pl.ANY)
    bf16, f32, dma = jnp.bfloat16, jnp.float32, pltpu.SemaphoreType.DMA
    return pl.pallas_call(
        kernel,
        out_shape=(outs, outs),
        in_specs=[anywhere] * 4 + [pl.BlockSpec(memory_space=pltpu.VMEM)],
        out_specs=(anywhere, anywhere),
        scratch_shapes=[
            pltpu.VMEM(w_qkv.shape[1:], bf16),
            pltpu.VMEM((4 * HD, cols), bf16),
            pltpu.VMEM((STAGES, 4, 2, ROWS, half_cols), bf16),
            pltpu.VMEM((STAGES, ROWS, 4 * HD), bf16),
            pltpu.VMEM((STAGES, 2, ROWS, half_cols), bf16),
            pltpu.VMEM((2 * ROWS, HD), bf16),
            pltpu.VMEM((2 * ROWS, HD), bf16),
            pltpu.VMEM((8, 1, half_cols), f32),
            pltpu.VMEM((ROWS, 3 * HD), f32),
            pltpu.VMEM((ROWS, HD), f32),
            dma((4,)), dma((2, 2)), dma, dma((4,)), dma((4,)), dma((4,)), dma((4,)),
            dma((STAGES, 2, 2)), dma((STAGES, 2, 2)), dma((STAGES, 2)), dma((STAGES, 2)),
            dma((STAGES, 3)), dma((STAGES, 3)), dma((STAGES, 2)), dma((STAGES, 2)),
            dma((STAGES, 2)), dma((STAGES, 2)), dma((STAGES, 2)), dma((2, 4)), dma((2,)),
        ],
        compiler_params=pltpu.CompilerParams(
            collective_id=0, has_side_effects=True, vmem_limit_bytes=48 << 20
        ),
        cost_estimate=pl.CostEstimate(flops=6 * 10**9, bytes_accessed=14 * 10**6, transcendentals=10**5),
    )(held, incoming, w_qkv, w_out, norm_gain)


def solution(mesh):
    placed = (
        P("section", "dp", None, "tp"),
        P(None, "dp", None, "tp"),
        P("section", None, "tp"),
        P("section", "tp", None),
        P("section", None),
    )
    return jax.shard_map(
        local,
        mesh=mesh,
        in_specs=placed,
        out_specs=(P(None, "section", "dp", None, "tp"), P(None, "section", "dp", None, "tp")),
        check_vma=False,
    )
```

```python
import functools

import jax
import jax.numpy as jnp
from jax import lax
from jax.experimental import pallas as pl
from jax.experimental.pallas import tpu as pltpu
from jax.sharding import PartitionSpec as P

HD = 128
EPS = 1e-05
ROWS = 64
STAGES = 8
MESH = pl.DeviceIdType.MESH


def kernel(
    held, incoming, w_qkv, w_out, gain, sec_out, sh_out,
    w_ref, wo, xg, mg, ob, ib, keys, vals, g32, acc, ssq,
    w_sem, x_sem, wol_sem, wo_s, wo_r, wx_s, wx_r,
    own_s, own_r, fw_s, fw_r, mix_s, mix_r, hop_s, hop_r, ret_s, ret_r, loc_s, il_sem, inc_s, inc_r, ip_s, ip_r,
):
    s, y, d = lax.axis_index("section"), lax.axis_index("tp"), lax.axis_index("dp")
    sections, tps = lax.axis_size("section"), 4
    half_cols = xg.shape[4]
    cols = 2 * half_cols

    def tp(o):
        return lax.rem(y + o, tps)

    right, left = {"tp": tp(1)}, {"tp": tp(3)}
    after = {"section": lax.rem(s + 1, sections)}
    before = {"section": lax.rem(s + sections - 1, sections)}

    def remote(src, dst, send, recv, to):
        return pltpu.make_async_remote_copy(
            src_ref=src, dst_ref=dst, send_sem=send, recv_sem=recv, device_id=to, device_id_type=MESH
        )

    own_rows = pl.ds(pl.multiple_of(y * HD, HD), HD)
    own_cols = pl.ds(pl.multiple_of(y * cols, cols), cols)
    wol = pltpu.make_async_copy(w_out.at[0, :, own_cols], wo.at[own_rows, :], wol_sem)

    def w_load(o):
        block = tp(o)
        rows = pl.ds(pl.multiple_of(block * cols, cols), cols)
        return pltpu.make_async_copy(w_qkv.at[0, rows, :], w_ref.at[rows, :], w_sem.at[o])

    def x_load(k, c):
        return pltpu.make_async_copy(
            held.at[0, 0, pl.ds(pl.multiple_of((k - 2) * ROWS, ROWS), ROWS), pl.ds(c * half_cols, half_cols)],
            xg.at[k, y, c],
            x_sem.at[k - 2, c],
        )

    for k in (2, 3):
        for c in range(2):
            x_load(k, c).start()
    for o in (0, 3, 1, 2):
        w_load(o).start()
    wol.start()

    helper = lax.rem(s, 4) == 0
    barrier = pltpu.get_barrier_semaphore()
    for to in ({"tp": tp(1)}, {"tp": tp(2)}, {"tp": tp(3)}, {"dp": 1 - d}, after, before):
        pl.semaphore_signal(barrier, inc=1, device_id=to, device_id_type=MESH)

    @pl.when(s == 0)
    def _():
        for j in range(1, 8):
            pl.semaphore_signal(barrier, inc=1, device_id={"section": 4 * j}, device_id_type=MESH)

    pl.semaphore_wait(barrier, jnp.where(jnp.logical_and(helper, s > 0), 7, 6))

    piece = cols // 8
    lane = pl.ds(pl.multiple_of((s // 4) * piece, piece), piece)

    def inc_load(h):
        return pltpu.make_async_copy(incoming.at[0, 0, pl.ds(h * ROWS, ROWS), lane], ib.at[h, y], il_sem.at[h])

    def inc_send(h, o):
        return remote(
            incoming.at[0, 0, pl.ds(h * ROWS, ROWS), lane], ib.at[h, y], inc_s.at[h, o - 1], inc_r.at[h, o - 1], {"tp": tp(o)}
        )

    def inc_place(h):
        j = s // 4
        return xg.at[h, :, j // 4, :, pl.ds(pl.multiple_of(lax.rem(j, 4) * piece, piece), piece)]

    def inc_pass(h):
        return remote(ib.at[h], inc_place(h), ip_s.at[h], ip_r.at[h], {"section": 0})

    def inc_keep(h):
        return pltpu.make_async_copy(ib.at[h], inc_place(h), ip_r.at[h])

    @pl.when(helper)
    def _():
        for h in range(2):
            for o in (2, 1, 3):
                inc_send(h, o).start()
            inc_load(h).start()

    def wo_send(o):
        there = pl.ds(pl.multiple_of(tp(o) * cols, cols), cols)
        mine = pl.ds(pl.multiple_of(y * HD + d * 64, 64), 64)
        return remote(
            w_out.at[0, pl.ds(pl.multiple_of(d * 64, 64), 64), there], wo.at[mine, :], wo_s.at[o], wo_r.at[o], {"tp": tp(o)}
        )

    def wo_pass(o):
        rows = pl.ds(pl.multiple_of(tp(4 - o) * HD + d * 64, 64), 64)
        return remote(wo.at[rows, :], wo.at[rows, :], wx_s.at[o], wx_r.at[o], {"dp": 1 - d})

    for o in (1, 3, 2):
        wo_send(o).start()

    def own_copy(k, way, c):
        block = xg.at[k, y, c]
        return remote(block, block, own_s.at[k, way, c], own_r.at[k, way, c], (right, left)[way])

    def own_arrival(k, way, c):
        block = xg.at[k, tp(3 if way == 0 else 1), c]
        return remote(block, block, own_s.at[k, way, c], own_r.at[k, way, c], (right, left)[way])

    def pass_on(k, way):
        block = xg.at[k, tp(3 if way == 0 else 1), way]
        return remote(block, block, fw_s.at[k, way], fw_r.at[k, way], (right, left)[way])

    def pass_arrival(k, way):
        block = xg.at[k, tp(2), way]
        return remote(block, block, fw_s.at[k, way], fw_r.at[k, way], (right, left)[way])

    @pl.when(helper)
    def _():
        for h in range(2):
            for o in (2, 1, 3):
                inc_send(h, o).wait_recv()
            inc_load(h).wait()

            @pl.when(s > 0)
            def _():
                inc_pass(h).start()

            @pl.when(s == 0)
            def _():
                inc_keep(h).start()

    for i in range(8):
        g32[i] = gain[:, i * half_cols:(i + 1) * half_cols].astype(jnp.float32)
    keys[...] = jnp.zeros_like(keys)
    vals[...] = jnp.zeros_like(vals)

    for o in (1, 3, 2):
        wo_send(o).wait_recv()
        wo_pass(o).start()
        if o == 3:
            for c in range(2):
                x_load(2, c).wait()
            for way, c in ((0, 0), (1, 1), (0, 1), (1, 0)):
                own_copy(2, way, c).start()

    def mix_copy(k, o):
        block = mg.at[k, :, pl.ds(pl.multiple_of(y * HD, HD), HD)]
        return remote(block, block, mix_s.at[k, o - 1], mix_r.at[k, o - 1], {"tp": tp(o)})

    def hop(k, c):
        to = jnp.where(k < 2, k + 6, k + 2)
        return remote(ob.at[k, c], xg.at[to, y, c], hop_s.at[k, c], hop_r.at[to, c], after)

    def hop_arrival(k, c):
        return remote(xg.at[k, y, c], xg.at[k, y, c], hop_s.at[k, c], hop_r.at[k, c], after)

    def out_at(ref, t, k, c):
        rows = pl.ds(pl.multiple_of(lax.rem(k, 2) * ROWS, ROWS), ROWS)
        return ref.at[t, 0, 0, rows, pl.ds(c * half_cols, half_cols)]

    def give_back(k, c):
        t = jnp.where(k < 6, 0, 1)
        return remote(ob.at[k, c], out_at(sh_out, t, k, c), ret_s.at[k, c], ret_r.at[k, c], before)

    def keep(k, c):
        t = jnp.where(k // 2 == 1, 0, 1)
        return pltpu.make_async_copy(ob.at[k, c], out_at(sec_out, t, k, c), loc_s.at[k, c])

    def goes_on(k):
        return jnp.logical_or(k < 4, jnp.logical_and(k < 6, s > 0))

    def multiply(k, block, c, first=False):
        index = block * 2 + c
        values = xg[k, block, c].astype(jnp.float32)
        rows = pl.ds(pl.multiple_of(index * half_cols, half_cols), half_cols)
        product = jnp.dot(
            (values * g32[index]).astype(jnp.bfloat16), w_ref[rows, :], preferred_element_type=jnp.float32
        )
        squares = values * values
        part = squares[:, :HD]
        for i in range(1, half_cols // HD):
            part = part + squares[:, i * HD:(i + 1) * HD]
        if first:
            acc[...] = product
            ssq[...] = part
        else:
            acc[...] += product
            ssq[...] += part

    def attend(k):
        gathered = k >= 2

        @pl.when(k == 2)
        def _():
            for o in range(4):
                w_load(o).wait()

        @pl.when(k < 2)
        def _():
            pltpu.make_async_copy(xg.at[k], xg.at[k], ip_r.at[k]).wait()

        multiply(k, y, 0, True)
        multiply(k, y, 1)
        for way in range(2):
            @pl.when(gathered)
            def _():
                own_arrival(k, way, way).wait_recv()
                pass_on(k, way).start()

            multiply(k, tp(3 if way == 0 else 1), way)
        for way in range(2):
            @pl.when(gathered)
            def _():
                own_arrival(k, way, 1 - way).wait_recv()

            multiply(k, tp(3 if way == 0 else 1), 1 - way)
        more = jnp.logical_and(gathered, k < 7)

        @pl.when(k == 2)
        def _():
            for c in range(2):
                x_load(3, c).wait()
                own_copy(3, c, c).start()

        @pl.when(jnp.logical_and(more, k > 2))
        def _():
            for c in range(2):
                hop_arrival(k + 1, c).wait_recv()
                own_copy(k + 1, c, c).start()

        for way in range(2):
            @pl.when(gathered)
            def _():
                pass_arrival(k, way).wait_recv()

            multiply(k, tp(2), way)

        half = lax.rem(k, 2)
        mean = jnp.sum(ssq[...], axis=1, keepdims=True) * (1.0 / (4 * cols))
        proj = (acc[...] * lax.rsqrt(mean + EPS)).astype(jnp.bfloat16)
        rows = pl.ds(pl.multiple_of(half * ROWS, ROWS), ROWS)
        kind = jnp.where(k < 2, 0, 1)
        keys[kind, rows, :] = proj[:, HD:2 * HD]
        vals[kind, rows, :] = proj[:, 2 * HD:]
        scores = lax.dot_general(
            proj[:, :HD], keys[kind], (((1,), (1,)), ((), ())), preferred_element_type=jnp.float32
        ) * HD ** (-0.5)
        at_row = lax.broadcasted_iota(jnp.int32, scores.shape, 0) + half * ROWS
        at_col = lax.broadcasted_iota(jnp.int32, scores.shape, 1)
        scores = jnp.where(at_col <= at_row, scores, -1e30)
        powers = jnp.exp(scores - jnp.max(scores, axis=1, keepdims=True))
        weights = (powers / jnp.sum(powers, axis=1, keepdims=True)).astype(jnp.bfloat16)
        mixed = jnp.dot(weights, vals[kind], preferred_element_type=jnp.float32).astype(jnp.bfloat16)
        mg[k, :, pl.ds(pl.multiple_of(y * HD, HD), HD)] = mixed
        for o in (2, 1, 3):
            mix_copy(k, o).start()

        @pl.when(more)
        def _():
            for c in range(2):
                own_copy(k + 1, c, 1 - c).start()

    def project(k):
        @pl.when(k == 2)
        def _():
            wol.wait()
            for o in (1, 3, 2):
                wo_pass(o).wait_recv()

        for o in (1, 3, 2):
            mix_copy(k, o).wait_recv()
        mixes = mg[k]
        for c in range(2):
            for i in range(2):
                n = half_cols // 2
                delta = jnp.dot(
                    mixes, wo[:, c * half_cols + i * n:c * half_cols + (i + 1) * n], preferred_element_type=jnp.float32
                )
                ob[k, c, :, i * n:(i + 1) * n] = (
                    xg[k, y, c, :, i * n:(i + 1) * n].astype(jnp.float32) + delta
                ).astype(jnp.bfloat16)

            @pl.when(goes_on(k))
            def _():
                hop(k, c).start()
                keep(k, c).start()

            @pl.when(k >= 4)
            def _():
                give_back(k, c).start()

    def step(k, carry):
        first = jnp.logical_and(k < 4, s == 0)

        def attend_one(i, c):
            attend(k - 2 * i)
            return c

        def project_one(i, c):
            project(jnp.where(i == 0, k, i - 1))
            return c

        lax.fori_loop(0, jnp.where(first, 2, 1), attend_one, 0)
        lax.fori_loop(0, jnp.where(jnp.logical_and(first, k == 3), 3, 1), project_one, 0)
        return carry

    lax.fori_loop(2, STAGES, step, 0)

    for o in (1, 3, 2):
        wo_send(o).wait_send()
        wo_pass(o).wait_send()

    @pl.when(helper)
    def _():
        for h in range(2):
            for o in (2, 1, 3):
                inc_send(h, o).wait_send()

            @pl.when(s > 0)
            def _():
                inc_pass(h).wait_send()

    def drain(k, carry):
        gathered = k >= 2

        @pl.when(gathered)
        def _():
            for way in range(2):
                for c in range(2):
                    own_copy(k, way, c).wait_send()
                pass_on(k, way).wait_send()

        @pl.when(jnp.logical_or(gathered, s == 0))
        def _():
            for o in (1, 2, 3):
                mix_copy(k, o).wait_send()

            @pl.when(goes_on(k))
            def _():
                for c in range(2):
                    hop(k, c).wait_send()
                    keep(k, c).wait()

        @pl.when(k >= 4)
        def _():
            for c in range(2):
                give_back(k, c).wait()

        return carry

    lax.fori_loop(0, STAGES, drain, 0)


def settle(a, b, c, d):
    c[...] = a[...]
    d[...] = b[...]


def local(held, incoming, w_qkv, w_out, norm_gain):
    cols = held.shape[3]
    half_cols = cols // 2
    outs = jax.ShapeDtypeStruct((2, 1, 1, held.shape[2], cols), jnp.bfloat16)
    anywhere = pl.BlockSpec(memory_space=pl.ANY)
    bf16, f32, dma = jnp.bfloat16, jnp.float32, pltpu.SemaphoreType.DMA
    results = pl.pallas_call(
        kernel,
        out_shape=(outs, outs),
        in_specs=[anywhere] * 4 + [pl.BlockSpec(memory_space=pltpu.VMEM)],
        out_specs=(anywhere, anywhere),
        scratch_shapes=[
            pltpu.VMEM(w_qkv.shape[1:], bf16),
            pltpu.VMEM((4 * HD, cols), bf16),
            pltpu.VMEM((STAGES, 4, 2, ROWS, half_cols), bf16),
            pltpu.VMEM((STAGES, ROWS, 4 * HD), bf16),
            pltpu.VMEM((STAGES, 2, ROWS, half_cols), bf16),
            pltpu.VMEM((2, 4, ROWS, cols // 8), bf16),
            pltpu.VMEM((2, 2 * ROWS, HD), bf16),
            pltpu.VMEM((2, 2 * ROWS, HD), bf16),
            pltpu.VMEM((8, 1, half_cols), f32),
            pltpu.VMEM((ROWS, 3 * HD), f32),
            pltpu.VMEM((ROWS, HD), f32),
            dma((4,)), dma((2, 2)), dma, dma((4,)), dma((4,)), dma((4,)), dma((4,)),
            dma((STAGES, 2, 2)), dma((STAGES, 2, 2)), dma((STAGES, 2)), dma((STAGES, 2)),
            dma((STAGES, 3)), dma((STAGES, 3)), dma((STAGES, 2)), dma((STAGES, 2)),
            dma((STAGES, 2)), dma((STAGES, 2)), dma((STAGES, 2)),
            dma((2,)), dma((2, 3)), dma((2, 3)), dma((2,)), dma((2,)),
        ],
        compiler_params=pltpu.CompilerParams(
            collective_id=0, has_side_effects=True, vmem_limit_bytes=60 << 20
        ),
        cost_estimate=pl.CostEstimate(flops=6 * 10**9, bytes_accessed=14 * 10**6, transcendentals=10**5),
    )(held, incoming, w_qkv, w_out, norm_gain)
    block = pl.BlockSpec((1, 1, 1, held.shape[2], cols), lambda t: (t, 0, 0, 0, 0))
    return pl.pallas_call(
        settle, out_shape=(outs, outs), grid=(2,), in_specs=[block] * 2, out_specs=(block, block)
    )(*results)


def solution(mesh):
    placed = (
        P("section", "dp", None, "tp"),
        P(None, "dp", None, "tp"),
        P("section", None, "tp"),
        P("section", "tp", None),
        P("section", None),
    )
    return jax.shard_map(
        local,
        mesh=mesh,
        in_specs=placed,
        out_specs=(P(None, "section", "dp", None, "tp"), P(None, "section", "dp", None, "tp")),
        check_vma=False,
    )
```

```python
import functools

import jax
import jax.numpy as jnp
from jax import lax
from jax.experimental import pallas as pl
from jax.experimental.pallas import tpu as pltpu
from jax.sharding import PartitionSpec as P

HD = 128
EPS = 1e-05
ROWS = 64
STAGES = 8
MESH = pl.DeviceIdType.MESH


def kernel(
    held, incoming, w_qkv, w_out, gain, sec_out, sh_out,
    w_ref, wo, xg, mg, ob, ib, keys, vals, g32, acc, ssq,
    w_sem, x_sem, wol_sem, wo_s, wo_r, wx_s, wx_r,
    own_s, own_r, fw_s, fw_r, mix_s, mix_r, hop_s, hop_r, ret_s, ret_r, loc_s, il_sem, inc_s, inc_r, ip_s, ip_r,
):
    s, y, d = lax.axis_index("section"), lax.axis_index("tp"), lax.axis_index("dp")
    sections, tps = lax.axis_size("section"), 4
    half_cols = xg.shape[4]
    cols = 2 * half_cols

    def tp(o):
        return lax.rem(y + o, tps)

    right, left = {"tp": tp(1)}, {"tp": tp(3)}
    after = {"section": lax.rem(s + 1, sections)}
    before = {"section": lax.rem(s + sections - 1, sections)}

    def remote(src, dst, send, recv, to):
        return pltpu.make_async_remote_copy(
            src_ref=src, dst_ref=dst, send_sem=send, recv_sem=recv, device_id=to, device_id_type=MESH
        )

    own_rows = pl.ds(pl.multiple_of(y * HD, HD), HD)
    own_cols = pl.ds(pl.multiple_of(y * cols, cols), cols)
    wol = pltpu.make_async_copy(w_out.at[0, :, own_cols], wo.at[own_rows, :], wol_sem)

    def w_load(o):
        block = tp(o)
        rows = pl.ds(pl.multiple_of(block * cols, cols), cols)
        return pltpu.make_async_copy(w_qkv.at[0, rows, :], w_ref.at[rows, :], w_sem.at[o])

    def x_load(k, c):
        return pltpu.make_async_copy(
            held.at[0, 0, pl.ds(pl.multiple_of((k - 2) * ROWS, ROWS), ROWS), pl.ds(c * half_cols, half_cols)],
            xg.at[k, y, c],
            x_sem.at[k - 2, c],
        )

    for k in (2, 3):
        for c in range(2):
            x_load(k, c).start()
    for o in (0, 3, 1, 2):
        w_load(o).start()
    wol.start()

    helper = lax.rem(s, 4) == 0
    barrier = pltpu.get_barrier_semaphore()
    for to in ({"tp": tp(1)}, {"tp": tp(2)}, {"tp": tp(3)}, {"dp": 1 - d}, after, before):
        pl.semaphore_signal(barrier, inc=1, device_id=to, device_id_type=MESH)

    @pl.when(s == 0)
    def _():
        for j in range(1, 8):
            pl.semaphore_signal(barrier, inc=1, device_id={"section": 4 * j}, device_id_type=MESH)

    pl.semaphore_wait(barrier, jnp.where(jnp.logical_and(helper, s > 0), 7, 6))

    piece = cols // 8
    lane = pl.ds(pl.multiple_of((s // 4) * piece, piece), piece)

    def inc_load(h):
        return pltpu.make_async_copy(incoming.at[0, 0, pl.ds(h * ROWS, ROWS), lane], ib.at[h, y], il_sem.at[h])

    def inc_send(h, o):
        return remote(
            incoming.at[0, 0, pl.ds(h * ROWS, ROWS), lane], ib.at[h, y], inc_s.at[h, o - 1], inc_r.at[h, o - 1], {"tp": tp(o)}
        )

    def inc_place(h):
        j = s // 4
        return xg.at[h, :, j // 4, :, pl.ds(pl.multiple_of(lax.rem(j, 4) * piece, piece), piece)]

    def inc_pass(h):
        return remote(ib.at[h], inc_place(h), ip_s.at[h], ip_r.at[h], {"section": 0})

    def inc_keep(h):
        return pltpu.make_async_copy(ib.at[h], inc_place(h), ip_r.at[h])

    @pl.when(helper)
    def _():
        for h in range(2):
            for o in (2, 1, 3):
                inc_send(h, o).start()
            inc_load(h).start()

    def wo_send(o):
        there = pl.ds(pl.multiple_of(tp(o) * cols, cols), cols)
        mine = pl.ds(pl.multiple_of(y * HD + d * 64, 64), 64)
        return remote(
            w_out.at[0, pl.ds(pl.multiple_of(d * 64, 64), 64), there], wo.at[mine, :], wo_s.at[o], wo_r.at[o], {"tp": tp(o)}
        )

    def wo_pass(o):
        rows = pl.ds(pl.multiple_of(tp(4 - o) * HD + d * 64, 64), 64)
        return remote(wo.at[rows, :], wo.at[rows, :], wx_s.at[o], wx_r.at[o], {"dp": 1 - d})

    for o in (1, 3, 2):
        wo_send(o).start()

    def own_copy(k, way, c):
        block = xg.at[k, y, c]
        return remote(block, block, own_s.at[k, way, c], own_r.at[k, way, c], (right, left)[way])

    def own_arrival(k, way, c):
        block = xg.at[k, tp(3 if way == 0 else 1), c]
        return remote(block, block, own_s.at[k, way, c], own_r.at[k, way, c], (right, left)[way])

    def pass_on(k, way):
        block = xg.at[k, tp(3 if way == 0 else 1), way]
        return remote(block, block, fw_s.at[k, way], fw_r.at[k, way], (right, left)[way])

    def pass_arrival(k, way):
        block = xg.at[k, tp(2), way]
        return remote(block, block, fw_s.at[k, way], fw_r.at[k, way], (right, left)[way])

    @pl.when(helper)
    def _():
        for h in range(2):
            for o in (2, 1, 3):
                inc_send(h, o).wait_recv()
            inc_load(h).wait()

            @pl.when(s > 0)
            def _():
                inc_pass(h).start()

            @pl.when(s == 0)
            def _():
                inc_keep(h).start()

    for i in range(8):
        g32[i] = gain[:, i * half_cols:(i + 1) * half_cols].astype(jnp.float32)
    keys[...] = jnp.zeros_like(keys)
    vals[...] = jnp.zeros_like(vals)

    for o in (1, 3, 2):
        wo_send(o).wait_recv()
        wo_pass(o).start()
        if o == 3:
            for c in range(2):
                x_load(2, c).wait()
            for way, c in ((0, 0), (1, 1), (0, 1), (1, 0)):
                own_copy(2, way, c).start()

    def mix_copy(k, o):
        block = mg.at[k, :, pl.ds(pl.multiple_of(y * HD, HD), HD)]
        return remote(block, block, mix_s.at[k, o - 1], mix_r.at[k, o - 1], {"tp": tp(o)})

    def hop(k, c):
        to = jnp.where(k < 2, k + 6, k + 2)
        return remote(ob.at[k, c], xg.at[to, y, c], hop_s.at[k, c], hop_r.at[to, c], after)

    def hop_arrival(k, c):
        return remote(xg.at[k, y, c], xg.at[k, y, c], hop_s.at[k, c], hop_r.at[k, c], after)

    def out_at(ref, t, k, c):
        rows = pl.ds(pl.multiple_of(lax.rem(k, 2) * ROWS, ROWS), ROWS)
        return ref.at[t, 0, 0, rows, pl.ds(c * half_cols, half_cols)]

    def give_back(k, c):
        t = jnp.where(k < 6, 0, 1)
        return remote(ob.at[k, c], out_at(sh_out, t, k, c), ret_s.at[k, c], ret_r.at[k, c], before)

    def keep(k, c):
        t = jnp.where(k // 2 == 1, 0, 1)
        return pltpu.make_async_copy(ob.at[k, c], out_at(sec_out, t, k, c), loc_s.at[k, c])

    def goes_on(k):
        return jnp.logical_or(k < 4, jnp.logical_and(k < 6, s > 0))

    def multiply(k, block, c, first=False):
        index = block * 2 + c
        values = xg[k, block, c].astype(jnp.float32)
        rows = pl.ds(pl.multiple_of(index * half_cols, half_cols), half_cols)
        product = jnp.dot(
            (values * g32[index]).astype(jnp.bfloat16), w_ref[rows, :], preferred_element_type=jnp.float32
        )
        squares = values * values
        part = squares[:, :HD]
        for i in range(1, half_cols // HD):
            part = part + squares[:, i * HD:(i + 1) * HD]
        if first:
            acc[...] = product
            ssq[...] = part
        else:
            acc[...] += product
            ssq[...] += part

    def attend(k):
        gathered = k >= 2

        @pl.when(k == 2)
        def _():
            for o in range(4):
                w_load(o).wait()

        @pl.when(k < 2)
        def _():
            pltpu.make_async_copy(xg.at[k], xg.at[k], ip_r.at[k]).wait()

        multiply(k, y, 0, True)
        multiply(k, y, 1)
        for way in range(2):
            @pl.when(gathered)
            def _():
                own_arrival(k, way, way).wait_recv()
                pass_on(k, way).start()

            multiply(k, tp(3 if way == 0 else 1), way)
        for way in range(2):
            @pl.when(gathered)
            def _():
                own_arrival(k, way, 1 - way).wait_recv()

            multiply(k, tp(3 if way == 0 else 1), 1 - way)
        @pl.when(k == 3)
        def _():
            project(2)

        more = jnp.logical_and(gathered, k < 7)

        @pl.when(k == 2)
        def _():
            for c in range(2):
                x_load(3, c).wait()
                own_copy(3, c, c).start()

        @pl.when(jnp.logical_and(more, k > 2))
        def _():
            for c in range(2):
                hop_arrival(k + 1, c).wait_recv()
                own_copy(k + 1, c, c).start()

        for way in range(2):
            @pl.when(gathered)
            def _():
                pass_arrival(k, way).wait_recv()

            multiply(k, tp(2), way)

        half = lax.rem(k, 2)
        mean = jnp.sum(ssq[...], axis=1, keepdims=True) * (1.0 / (4 * cols))
        proj = (acc[...] * lax.rsqrt(mean + EPS)).astype(jnp.bfloat16)
        rows = pl.ds(pl.multiple_of(half * ROWS, ROWS), ROWS)
        kind = jnp.where(k < 2, 0, 1)
        keys[kind, rows, :] = proj[:, HD:2 * HD]
        vals[kind, rows, :] = proj[:, 2 * HD:]
        scores = lax.dot_general(
            proj[:, :HD], keys[kind], (((1,), (1,)), ((), ())), preferred_element_type=jnp.float32
        ) * HD ** (-0.5)
        at_row = lax.broadcasted_iota(jnp.int32, scores.shape, 0) + half * ROWS
        at_col = lax.broadcasted_iota(jnp.int32, scores.shape, 1)
        scores = jnp.where(at_col <= at_row, scores, -1e30)
        powers = jnp.exp(scores - jnp.max(scores, axis=1, keepdims=True))
        weights = (powers / jnp.sum(powers, axis=1, keepdims=True)).astype(jnp.bfloat16)
        mixed = jnp.dot(weights, vals[kind], preferred_element_type=jnp.float32).astype(jnp.bfloat16)
        mg[k, :, pl.ds(pl.multiple_of(y * HD, HD), HD)] = mixed
        for o in (2, 1, 3):
            mix_copy(k, o).start()

        @pl.when(more)
        def _():
            for c in range(2):
                own_copy(k + 1, c, 1 - c).start()

    def project(k):
        @pl.when(k == 2)
        def _():
            wol.wait()
            for o in (1, 3, 2):
                wo_pass(o).wait_recv()

        for o in (1, 3, 2):
            mix_copy(k, o).wait_recv()
        mixes = mg[k]
        for c in range(2):
            for i in range(2):
                n = half_cols // 2
                delta = jnp.dot(
                    mixes, wo[:, c * half_cols + i * n:c * half_cols + (i + 1) * n], preferred_element_type=jnp.float32
                )
                ob[k, c, :, i * n:(i + 1) * n] = (
                    xg[k, y, c, :, i * n:(i + 1) * n].astype(jnp.float32) + delta
                ).astype(jnp.bfloat16)

            @pl.when(goes_on(k))
            def _():
                hop(k, c).start()
                keep(k, c).start()

            @pl.when(k >= 4)
            def _():
                give_back(k, c).start()

    def step(k, carry):
        first = jnp.logical_and(k < 4, s == 0)

        def attend_one(i, c):
            attend(k - 2 * i)
            return c

        def project_one(i, c):
            project(jnp.where(i == 0, k, i - 1))
            return c

        lax.fori_loop(0, jnp.where(first, 2, 1), attend_one, 0)
        lax.fori_loop(0, jnp.where(k == 2, 0, jnp.where(jnp.logical_and(first, k == 3), 3, 1)), project_one, 0)
        return carry

    lax.fori_loop(2, STAGES, step, 0)

    for o in (1, 3, 2):
        wo_send(o).wait_send()
        wo_pass(o).wait_send()

    @pl.when(helper)
    def _():
        for h in range(2):
            for o in (2, 1, 3):
                inc_send(h, o).wait_send()

            @pl.when(s > 0)
            def _():
                inc_pass(h).wait_send()

    def drain(k, carry):
        gathered = k >= 2

        @pl.when(gathered)
        def _():
            for way in range(2):
                for c in range(2):
                    own_copy(k, way, c).wait_send()
                pass_on(k, way).wait_send()

        @pl.when(jnp.logical_or(gathered, s == 0))
        def _():
            for o in (1, 2, 3):
                mix_copy(k, o).wait_send()

            @pl.when(goes_on(k))
            def _():
                for c in range(2):
                    hop(k, c).wait_send()
                    keep(k, c).wait()

        @pl.when(k >= 4)
        def _():
            for c in range(2):
                give_back(k, c).wait()

        return carry

    lax.fori_loop(0, STAGES, drain, 0)


def settle(a, b, c, d):
    c[...] = a[...]
    d[...] = b[...]


def local(held, incoming, w_qkv, w_out, norm_gain):
    cols = held.shape[3]
    half_cols = cols // 2
    outs = jax.ShapeDtypeStruct((2, 1, 1, held.shape[2], cols), jnp.bfloat16)
    anywhere = pl.BlockSpec(memory_space=pl.ANY)
    bf16, f32, dma = jnp.bfloat16, jnp.float32, pltpu.SemaphoreType.DMA
    results = pl.pallas_call(
        kernel,
        out_shape=(outs, outs),
        in_specs=[anywhere] * 4 + [pl.BlockSpec(memory_space=pltpu.VMEM)],
        out_specs=(anywhere, anywhere),
        scratch_shapes=[
            pltpu.VMEM(w_qkv.shape[1:], bf16),
            pltpu.VMEM((4 * HD, cols), bf16),
            pltpu.VMEM((STAGES, 4, 2, ROWS, half_cols), bf16),
            pltpu.VMEM((STAGES, ROWS, 4 * HD), bf16),
            pltpu.VMEM((STAGES, 2, ROWS, half_cols), bf16),
            pltpu.VMEM((2, 4, ROWS, cols // 8), bf16),
            pltpu.VMEM((2, 2 * ROWS, HD), bf16),
            pltpu.VMEM((2, 2 * ROWS, HD), bf16),
            pltpu.VMEM((8, 1, half_cols), f32),
            pltpu.VMEM((ROWS, 3 * HD), f32),
            pltpu.VMEM((ROWS, HD), f32),
            dma((4,)), dma((2, 2)), dma, dma((4,)), dma((4,)), dma((4,)), dma((4,)),
            dma((STAGES, 2, 2)), dma((STAGES, 2, 2)), dma((STAGES, 2)), dma((STAGES, 2)),
            dma((STAGES, 3)), dma((STAGES, 3)), dma((STAGES, 2)), dma((STAGES, 2)),
            dma((STAGES, 2)), dma((STAGES, 2)), dma((STAGES, 2)),
            dma((2,)), dma((2, 3)), dma((2, 3)), dma((2,)), dma((2,)),
        ],
        compiler_params=pltpu.CompilerParams(
            collective_id=0, has_side_effects=True, vmem_limit_bytes=60 << 20
        ),
        cost_estimate=pl.CostEstimate(flops=6 * 10**9, bytes_accessed=14 * 10**6, transcendentals=10**5),
    )(held, incoming, w_qkv, w_out, norm_gain)
    block = pl.BlockSpec((1, 1, 1, ROWS, cols), lambda t, r: (t, 0, 0, r, 0))
    return pl.pallas_call(
        settle, out_shape=(outs, outs), grid=(2, held.shape[2] // ROWS), in_specs=[block] * 2, out_specs=(block, block)
    )(*results)


def solution(mesh):
    placed = (
        P("section", "dp", None, "tp"),
        P(None, "dp", None, "tp"),
        P("section", None, "tp"),
        P("section", "tp", None),
        P("section", None),
    )
    return jax.shard_map(
        local,
        mesh=mesh,
        in_specs=placed,
        out_specs=(P(None, "section", "dp", None, "tp"), P(None, "section", "dp", None, "tp")),
        check_vma=False,
    )
```
